256 devices in a mesh: minor: 8 (over z), major: 32 (over y, x, core).
Axes of the slice: x: 4, y: 4, z: 8, core: 2. Of those that a mesh axis runs over, the one named last changes fastest.
Arguments:
- queries: bfloat16 [131072, 1024], P(('major', 'minor')), may hold values from -1.75 to 1.75
- keys: bfloat16 [131072, 1024], P(('major', 'minor')), may hold values from -1.75 to 1.75
- values: bfloat16 [131072, 1024], P(('major', 'minor')), may hold values from -1.75 to 1.75
- cotangent: bfloat16 [131072, 1024], P(('major', 'minor')), may hold values from -1.75 to 1.75
Outputs:
- attended: bfloat16 [131072, 1024], P(('major', 'minor'))
- grad_queries: bfloat16 [131072, 1024], P(('major', 'minor'))
- grad_keys: bfloat16 [131072, 1024], P(('major', 'minor'))
- grad_values: bfloat16 [131072, 1024], P(('major', 'minor'))
The draws below stay inside these ranges and needn't reach their ends.
All inputs are finite; a program needn't handle non-finite values.
Results may differ from the reference program's by a relative error of at most 0.0057.
Values sent between devices are 32-bit elements; how exact they have to be, the bound alone decides.
A program may use at most 128 MiB of HBM per device.

```python
import jax
import jax.numpy as jnp
from jax import lax

H = 16
HD = 64
TOK_DEV = 512
TOKENS = 131072


def shard_levels(own_key, extent, pieces, least, top_value):
    loudness = 1.0
    for dim, shards_of in pieces:
        draws = jax.random.uniform(jax.random.fold_in(jax.random.fold_in(own_key, 6), dim), (shards_of,), jnp.float32, least / len(pieces), top_value / len(pieces))
        loudness = loudness * jnp.repeat(jnp.exp(draws), extent[dim] // shards_of).reshape((-1,) + (1,) * (len(extent) - 1 - dim))
    return loudness


def scatter_about(key, extent, deviation, limit, cuts=(), kind=jnp.bfloat16):
    values = deviation * jax.random.normal(key, extent, jnp.float32)
    if cuts:
        values = values * shard_levels(key, extent, cuts, -0.22, 0.18)
    return jnp.clip(values, -limit, limit).astype(kind)


def setup_inputs(seed: int = 0) -> dict:
    key_of = jax.random.split(jax.random.key(seed), 5)
    queries = scatter_about(key_of[0], (TOKENS, H * HD), 0.3, 1.75, ((0, 256),))
    keys = scatter_about(key_of[1], (TOKENS, H * HD), 0.3, 1.75, ((0, 256),))
    values = scatter_about(key_of[2], (TOKENS, H * HD), 0.3, 1.75, ((0, 256),))
    cotangent = scatter_about(key_of[3], (TOKENS, H * HD), 0.3, 1.75, ((0, 256),))
    return dict(queries=queries, keys=keys, values=values, cotangent=cotangent)


def block_terms(qb, kb, vb, gb, s_in, r_in, pos):
    rows = qb.shape[0]
    scale = 1.0 / jnp.sqrt(pos + 1.0)
    qf = qb.reshape(rows, H, HD).astype(jnp.float32)
    kf = kb.reshape(rows, H, HD).astype(jnp.float32)
    vf = vb.reshape(rows, H, HD).astype(jnp.float32)
    gf = gb.reshape(rows, H, HD).astype(jnp.float32)
    mask = (jnp.arange(rows)[:, None] >= jnp.arange(rows)[None, :])[None]
    scores = jnp.einsum('thd,shd->hts', qf, kf)
    weights = jnp.where(mask, scores * scale[None, :, None], 0.0).astype(jnp.bfloat16).astype(jnp.float32)
    backs = jnp.einsum('thd,shd->hts', gf, vf)
    back = jnp.where(mask, backs * scale[None, :, None], 0.0).astype(jnp.bfloat16).astype(jnp.float32)
    s_b = s_in.astype(jnp.bfloat16).astype(jnp.float32)
    r_b = r_in.astype(jnp.bfloat16).astype(jnp.float32)
    attended = jnp.einsum('hts,shd->thd', weights, vf) + scale[:, None, None] * jnp.einsum('thi,hij->thj', qf, s_b)
    grad_q = jnp.einsum('hts,shd->thd', back, kf) + scale[:, None, None] * jnp.einsum('thj,hij->thi', gf, s_b)
    grad_k = jnp.einsum('hts,thd->shd', back, qf) + jnp.einsum('shj,hij->shi', vf, r_b)
    grad_v = jnp.einsum('hts,thd->shd', weights, gf) + jnp.einsum('shi,hij->shj', kf, r_b)
    shaped = [x.reshape(rows, H * HD).astype(jnp.bfloat16) for x in (attended, grad_q, grad_k, grad_v)]
    return tuple(shaped)

def local_states(qb, kb, vb, gb, pos):
    rows = qb.shape[0]
    scale = 1.0 / jnp.sqrt(pos + 1.0)
    qf = qb.reshape(rows, H, HD).astype(jnp.float32)
    kf = kb.reshape(rows, H, HD).astype(jnp.float32)
    vf = vb.reshape(rows, H, HD).astype(jnp.float32)
    gf = gb.reshape(rows, H, HD).astype(jnp.float32)
    qc = (qf * scale[:, None, None]).astype(jnp.bfloat16).astype(jnp.float32)
    state = jnp.einsum('thi,thj->hij', kf, vf)
    adjoint = jnp.einsum('thi,thj->hij', qc, gf)
    return (state, adjoint)

def reference(queries, keys, values, cotangent):
    blocks = TOKENS // TOK_DEV
    split = lambda a: a.reshape(blocks, TOK_DEV, H * HD)
    qs, ks, vs, gs = (split(queries), split(keys), split(values), split(cotangent))
    starts = jnp.arange(blocks, dtype=jnp.int32)

    def position(index):
        return (index * TOK_DEV + jnp.arange(TOK_DEV, dtype=jnp.int32)).astype(jnp.float32)

    def states_of(item):
        qb, kb, vb, gb, index = item
        return local_states(qb, kb, vb, gb, position(index))
    s_all, r_all = lax.map(states_of, (qs, ks, vs, gs, starts))
    zero = jnp.zeros((H, HD, HD), jnp.float32)

    def accumulate(carry, term):
        return (carry + term, carry)
    _, s_in = lax.scan(accumulate, zero, s_all)
    _, r_in = lax.scan(accumulate, zero, r_all, reverse=True)

    def outputs_of(item):
        qb, kb, vb, gb, s_b, r_b, index = item
        return block_terms(qb, kb, vb, gb, s_b, r_b, position(index))
    results = lax.map(outputs_of, (qs, ks, vs, gs, s_in, r_in, starts))
    merged = [x.reshape(TOKENS, H * HD) for x in results]
    return (merged[0], merged[1], merged[2], merged[3])
```

```python
import functools

import jax
import jax.numpy as jnp
from jax import lax
from jax.experimental import pallas as pl
from jax.experimental.pallas import tpu as pltpu
from jax.sharding import PartitionSpec as P

TOK = 512
COLS = 1024
PAIRS = 8
CHUNK = 128
CHUNKS = TOK // CHUNK
F32 = jnp.float32
BF16 = jnp.bfloat16
MESH = pl.DeviceIdType.MESH

NT = (((1,), (1,)), ((), ()))
NN = (((1,), (0,)), ((), ()))
TN = (((0,), (0,)), ((), ()))


def dot(a, b, dims):
    return lax.dot_general(a, b, dims, preferred_element_type=F32)


def lanes_of(pair):
    return pl.ds(pl.multiple_of(pair * 128, 128), 128)


def token_scale(block, shape):
    pos = block * TOK + lax.broadcasted_iota(jnp.int32, shape, 0)
    return 1.0 / jnp.sqrt(pos.astype(F32) + 1.0)


def both_heads(x):
    low = lax.broadcasted_iota(jnp.int32, x.shape, 1) < 64
    zero = jnp.zeros_like(x)
    return jnp.concatenate([jnp.where(low, x, zero), jnp.where(low, zero, x)], axis=0)


def diagonal(x):
    row = lax.broadcasted_iota(jnp.int32, x.shape, 0) < 64
    col = lax.broadcasted_iota(jnp.int32, x.shape, 1) < 64
    return jnp.where(row == col, x, jnp.zeros_like(x))


def compact(x):
    low = lax.broadcasted_iota(jnp.int32, (64, 128), 1) < 64
    return jnp.where(low, x[0:64], x[64:128])


def states_kernel(
    q_hbm, k_hbm, v_hbm, g_hbm, part_hbm, state_hbm,
    q, k, v, g, qc, gc, scale, part, send, fwd, total, plane, ret, back,
    in_sem, out_sem, state_sem, fs_sem, fr_sem, ps_sem, pr_sem, rs_sem, rr_sem,
):
    z = lax.axis_index("minor")
    group = lax.axis_index("major")
    core = lax.rem(group, 2)
    chip = group // 2
    mine = core * 8 + z
    owned = z * 2 + core

    def column(step):
        return lax.rem(z + step // 2, 8), lax.rem(core + step % 2, 2)

    loads = [
        pltpu.make_async_copy(src, dst, in_sem.at[i])
        for i, (src, dst) in enumerate(((k_hbm, k), (v_hbm, v), (q_hbm, q), (g_hbm, g)))
    ]
    for load in loads:
        load.start()

    barrier = pltpu.get_barrier_semaphore()
    for step in range(1, 16):
        to_z, to_core = column(step)
        pl.semaphore_signal(
            barrier, inc=1, device_id={"minor": to_z, "major": chip * 2 + to_core}, device_id_type=MESH
        )
        other = lax.rem(chip + step, 16)
        pl.semaphore_signal(
            barrier, inc=1, device_id={"minor": z, "major": other * 2 + core}, device_id_type=MESH
        )

    scale[...] = token_scale(group * 8 + z, (TOK, 128))
    loads[0].wait()
    loads[1].wait()

    def key_states(p, _):
        at = lanes_of(p)
        s = compact(dot(k[:, at], v[:, at], TN))
        send[2 * p, 0:32] = s[0:32]
        send[2 * p + 1, 0:32] = s[32:64]
        return 0

    lax.fori_loop(0, PAIRS, key_states, 0)
    loads[2].wait()
    loads[3].wait()

    def query_states(p, _):
        at = lanes_of(p)
        c = scale[...]
        scaled = (q[:, at].astype(F32) * c).astype(BF16)
        qc[:, at] = scaled
        gc[:, at] = (g[:, at].astype(F32) * c).astype(BF16)
        r = compact(dot(scaled, g[:, at], TN))
        send[2 * p, 32:64] = r[0:32]
        send[2 * p + 1, 32:64] = r[32:64]
        return 0

    lax.fori_loop(0, PAIRS, query_states, 0)
    pl.semaphore_wait(barrier, 30)

    def forward(step):
        to_z, to_core = column(step)
        return pltpu.make_async_remote_copy(
            src_ref=send.at[to_z * 2 + to_core],
            dst_ref=fwd.at[mine],
            send_sem=fs_sem.at[step],
            recv_sem=fr_sem.at[mine],
            device_id={"minor": to_z, "major": chip * 2 + to_core},
            device_id_type=MESH,
        )

    def landed(step):
        from_z, from_core = column(step)
        slot = from_core * 8 + from_z
        return pltpu.make_async_remote_copy(
            src_ref=send.at[0],
            dst_ref=fwd.at[slot],
            send_sem=fs_sem.at[step],
            recv_sem=fr_sem.at[slot],
            device_id={"minor": from_z, "major": chip * 2 + from_core},
            device_id_type=MESH,
        )

    for step in range(1, 16):
        forward(step).start()
    fwd[mine] = send[owned]

    def inside(p, _):
        at = lanes_of(p)
        causal = lax.broadcasted_iota(jnp.int32, (CHUNK, 2 * CHUNK), 0) >= (
            lax.broadcasted_iota(jnp.int32, (CHUNK, 2 * CHUNK), 1) % CHUNK
        )
        state = None
        adjoints = []
        for n in range(CHUNKS):
            rows = pl.ds(n * CHUNK, CHUNK)
            adjoints.append(dot(qc[rows, at], g[rows, at], TN) if n else None)
        later = [None] * CHUNKS
        running = None
        for n in reversed(range(1, CHUNKS)):
            running = adjoints[n] if running is None else running + adjoints[n]
            later[n - 1] = running
        for n in range(CHUNKS):
            rows = pl.ds(n * CHUNK, CHUNK)
            q_n, k_n, v_n, g_n = q[rows, at], k[rows, at], v[rows, at], g[rows, at]
            qc_n, gc_n = qc[rows, at], gc[rows, at]
            k_two, v_two = both_heads(k_n), both_heads(v_n)
            q_two, g_two = both_heads(q_n), both_heads(g_n)
            weights = jnp.where(causal, dot(qc_n, k_two, NT), 0.0).astype(BF16)
            backs = jnp.where(causal, dot(gc_n, v_two, NT), 0.0).astype(BF16)
            w_rows = jnp.concatenate([weights[:, :CHUNK], weights[:, CHUNK:]], axis=0)
            b_rows = jnp.concatenate([backs[:, :CHUNK], backs[:, CHUNK:]], axis=0)
            attended = dot(weights, v_two, NN)
            grad_q = dot(backs, k_two, NN)
            grad_k = dot(b_rows, q_two, TN)
            grad_v = dot(w_rows, g_two, TN)
            if n:
                s = diagonal(state).astype(BF16)
                attended = attended + dot(qc_n, s, NN)
                grad_q = grad_q + dot(gc_n, s, NT)
            if n < CHUNKS - 1:
                r = diagonal(later[n]).astype(BF16)
                grad_k = grad_k + dot(v_n, r, NT)
                grad_v = grad_v + dot(k_n, r, NN)
                more = dot(k_n, v_n, TN)
                state = more if state is None else state + more
            for i, x in enumerate((attended, grad_q, grad_k, grad_v)):
                part[p, i, rows] = x
        pltpu.make_async_copy(part.at[p], part_hbm.at[p], out_sem.at[p]).start()
        return 0

    lax.fori_loop(0, 4, inside, 0)

    for step in range(1, 16):
        landed(step).wait_recv()
    run = jnp.zeros((32, 128), F32)
    for d in range(16):
        ret[d, 0:32] = run
        run = run + fwd[d, 0:32]
    total[0] = run
    run = jnp.zeros((32, 128), F32)
    for d in reversed(range(16)):
        ret[d, 32:64] = run
        run = run + fwd[d, 32:64]
    total[1] = run

    def across(step):
        other = lax.rem(chip + step, 16)
        return pltpu.make_async_remote_copy(
            src_ref=total.at[jnp.where(other > chip, 0, 1)],
            dst_ref=plane.at[chip],
            send_sem=ps_sem.at[step],
            recv_sem=pr_sem.at[chip],
            device_id={"minor": z, "major": other * 2 + core},
            device_id_type=MESH,
        )

    def crossed(step):
        other = lax.rem(chip + step, 16)
        return pltpu.make_async_remote_copy(
            src_ref=total.at[0],
            dst_ref=plane.at[other],
            send_sem=ps_sem.at[step],
            recv_sem=pr_sem.at[other],
            device_id={"minor": z, "major": other * 2 + core},
            device_id_type=MESH,
        )

    for step in range(1, 16):
        across(step).start()
    plane[chip] = jnp.zeros((32, 128), F32)

    lax.fori_loop(4, 6, inside, 0)

    for step in range(1, 16):
        crossed(step).wait_recv()
    before = jnp.zeros((32, 128), F32)
    after = jnp.zeros((32, 128), F32)
    for n in range(16):
        piece = plane[n]
        before = before + jnp.where(n < chip, piece, 0.0)
        after = after + jnp.where(n > chip, piece, 0.0)
    for d in range(16):
        ret[d, 0:32] = ret[d, 0:32] + before
        ret[d, 32:64] = ret[d, 32:64] + after

    def returned(step):
        to_z, to_core = column(step)
        return pltpu.make_async_remote_copy(
            src_ref=ret.at[to_core * 8 + to_z],
            dst_ref=back.at[owned],
            send_sem=rs_sem.at[step],
            recv_sem=rr_sem.at[owned],
            device_id={"minor": to_z, "major": chip * 2 + to_core},
            device_id_type=MESH,
        )

    def arrived(step):
        from_z, from_core = column(step)
        slot = from_z * 2 + from_core
        return pltpu.make_async_remote_copy(
            src_ref=ret.at[0],
            dst_ref=back.at[slot],
            send_sem=rs_sem.at[step],
            recv_sem=rr_sem.at[slot],
            device_id={"minor": from_z, "major": chip * 2 + from_core},
            device_id_type=MESH,
        )

    for step in range(1, 16):
        returned(step).start()
    back[owned] = ret[mine]

    lax.fori_loop(6, 8, inside, 0)

    for step in range(1, 16):
        arrived(step).wait_recv()
    out = pltpu.make_async_copy(back, state_hbm, state_sem)
    out.start()
    for step in range(1, 16):
        forward(step).wait_send()
        across(step).wait_send()
        returned(step).wait_send()

    def stored(p, _):
        pltpu.make_async_copy(part.at[p], part_hbm.at[p], out_sem.at[p]).wait()
        return 0

    lax.fori_loop(0, PAIRS, stored, 0)
    out.wait()


def finish_kernel(q, k, v, g, part, state, attended, grad_q, grad_k, grad_v):
    block = lax.axis_index("major") * 8 + lax.axis_index("minor")
    c = token_scale(block, (TOK, 128))
    s = jnp.concatenate([state[0, 0:32], state[1, 0:32]] * 2, axis=0)
    r = jnp.concatenate([state[0, 32:64], state[1, 32:64]] * 2, axis=0)
    s = diagonal(s).astype(BF16)
    r = diagonal(r).astype(BF16)
    attended[...] = (part[0, 0] + c * dot(q[...], s, NN)).astype(BF16)
    grad_q[...] = (part[0, 1] + c * dot(g[...], s, NT)).astype(BF16)
    grad_k[...] = (part[0, 2] + dot(v[...], r, NT)).astype(BF16)
    grad_v[...] = (part[0, 3] + dot(k[...], r, NN)).astype(BF16)


def on_device(queries, keys, values, cotangent):
    hbm = pl.BlockSpec(memory_space=pl.ANY)
    dma = pltpu.SemaphoreType.DMA
    part, state = pl.pallas_call(
        states_kernel,
        name="states",
        out_shape=(
            jax.ShapeDtypeStruct((PAIRS, 4, TOK, 128), F32),
            jax.ShapeDtypeStruct((16, 64, 128), F32),
        ),
        in_specs=[hbm] * 4,
        out_specs=(hbm, hbm),
        scratch_shapes=[
            pltpu.VMEM((TOK, COLS), BF16),
            pltpu.VMEM((TOK, COLS), BF16),
            pltpu.VMEM((TOK, COLS), BF16),
            pltpu.VMEM((TOK, COLS), BF16),
            pltpu.VMEM((TOK, COLS), BF16),
            pltpu.VMEM((TOK, COLS), BF16),
            pltpu.VMEM((TOK, 128), F32),
            pltpu.VMEM((PAIRS, 4, TOK, 128), F32),
            pltpu.VMEM((16, 64, 128), F32),
            pltpu.VMEM((16, 64, 128), F32),
            pltpu.VMEM((2, 32, 128), F32),
            pltpu.VMEM((16, 32, 128), F32),
            pltpu.VMEM((16, 64, 128), F32),
            pltpu.VMEM((16, 64, 128), F32),
            dma((4,)),
            dma((PAIRS,)),
            dma,
            dma((16,)),
            dma((16,)),
            dma((16,)),
            dma((16,)),
            dma((16,)),
            dma((16,)),
        ],
        compiler_params=pltpu.CompilerParams(
            collective_id=0, has_side_effects=True, vmem_limit_bytes=40 << 20
        ),
    )(queries, keys, values, cotangent)
    cols = pl.BlockSpec((TOK, 128), lambda p: (0, p))
    out = jax.ShapeDtypeStruct((TOK, COLS), BF16)
    return pl.pallas_call(
        finish_kernel,
        name="finish",
        grid=(PAIRS,),
        out_shape=(out,) * 4,
        in_specs=[cols] * 4
        + [
            pl.BlockSpec((1, 4, TOK, 128), lambda p: (p, 0, 0, 0)),
            pl.BlockSpec((2, 64, 128), lambda p: (p, 0, 0)),
        ],
        out_specs=(cols,) * 4,
        compiler_params=pltpu.CompilerParams(vmem_limit_bytes=40 << 20),
    )(queries, keys, values, cotangent, part, state)


def solution(mesh):
    placed = P(("major", "minor"), None)
    return jax.shard_map(
        on_device, mesh=mesh, in_specs=(placed,) * 4, out_specs=(placed,) * 4, check_vma=False
    )
```

```python
import jax
import jax.numpy as jnp
from jax import lax
from jax.experimental import pallas as pl
from jax.experimental.pallas import tpu as pltpu
from jax.sharding import PartitionSpec as P

TOK = 512
COLS = 1024
PAIRS = 8
CHUNK = 128
CHUNKS = TOK // CHUNK
F32 = jnp.float32
BF16 = jnp.bfloat16
MESH = pl.DeviceIdType.MESH

NT = (((1,), (1,)), ((), ()))
NN = (((1,), (0,)), ((), ()))
TN = (((0,), (0,)), ((), ()))


def dot(a, b, dims):
    return lax.dot_general(a, b, dims, preferred_element_type=F32)


def lanes_of(pair):
    return pl.ds(pl.multiple_of(pair * 128, 128), 128)


def token_scale(block, shape):
    pos = block * TOK + lax.broadcasted_iota(jnp.int32, shape, 0)
    return 1.0 / jnp.sqrt(pos.astype(F32) + 1.0)


def both_heads(x):
    low = lax.broadcasted_iota(jnp.int32, x.shape, 1) < 64
    zero = jnp.zeros_like(x)
    return jnp.concatenate([jnp.where(low, x, zero), jnp.where(low, zero, x)], axis=0)


def diagonal(x):
    row = lax.broadcasted_iota(jnp.int32, x.shape, 0) < 64
    col = lax.broadcasted_iota(jnp.int32, x.shape, 1) < 64
    return jnp.where(row == col, x, jnp.zeros_like(x))


def compact(x):
    low = lax.broadcasted_iota(jnp.int32, (64, 128), 1) < 64
    return jnp.where(low, x[0:64], x[64:128])


def attention_kernel(
    q_hbm, k_hbm, v_hbm, g_hbm, attended, grad_q, grad_k, grad_v,
    q, k, v, g, qc, gc, scale, part, send, fwd, total, plane, ret, back,
    in_sem, fs_sem, fr_sem, ps_sem, pr_sem, rs_sem, rr_sem,
):
    z = lax.axis_index("minor")
    group = lax.axis_index("major")
    core = lax.rem(group, 2)
    chip = group // 2
    mine = core * 8 + z
    owned = z * 2 + core
    zeros = jnp.zeros((32, 128), F32)

    def column(step):
        return lax.rem(z + step // 2, 8), lax.rem(core + step % 2, 2)

    loads = [
        pltpu.make_async_copy(src, dst, in_sem.at[i])
        for i, (src, dst) in enumerate(((k_hbm, k), (v_hbm, v), (q_hbm, q), (g_hbm, g)))
    ]
    for load in loads:
        load.start()

    barrier = pltpu.get_barrier_semaphore()
    for step in range(1, 16):
        to_z, to_core = column(step)
        pl.semaphore_signal(
            barrier, inc=1, device_id={"minor": to_z, "major": chip * 2 + to_core}, device_id_type=MESH
        )
        other = lax.rem(chip + step, 16)
        pl.semaphore_signal(
            barrier, inc=1, device_id={"minor": z, "major": other * 2 + core}, device_id_type=MESH
        )

    def forward(kind, step, peer):
        to_z, to_core = column(step)
        slot = to_core * 8 + to_z if peer else mine
        return pltpu.make_async_remote_copy(
            src_ref=send.at[kind, to_z * 2 + to_core],
            dst_ref=fwd.at[kind, slot],
            send_sem=fs_sem.at[kind, step],
            recv_sem=fr_sem.at[kind, slot],
            device_id={"minor": to_z, "major": chip * 2 + to_core},
            device_id_type=MESH,
        )

    def across(kind, step, peer):
        other = lax.rem(chip + step, 16)
        slot = other if peer else chip
        return pltpu.make_async_remote_copy(
            src_ref=total.at[kind],
            dst_ref=plane.at[kind, slot],
            send_sem=ps_sem.at[kind, step],
            recv_sem=pr_sem.at[kind, slot],
            device_id={"minor": z, "major": other * 2 + core},
            device_id_type=MESH,
        )

    def returned(kind, step, peer):
        to_z, to_core = column(step)
        slot = to_z * 2 + to_core if peer else owned
        return pltpu.make_async_remote_copy(
            src_ref=ret.at[kind, to_core * 8 + to_z],
            dst_ref=back.at[kind, slot],
            send_sem=rs_sem.at[kind, step],
            recv_sem=rr_sem.at[kind, slot],
            device_id={"minor": to_z, "major": chip * 2 + to_core},
            device_id_type=MESH,
        )

    def ahead(kind, step):
        other = lax.rem(chip + step, 16)
        return other > chip if kind == 0 else other < chip

    def send_slices(kind):
        for step in range(1, 16):
            forward(kind, step, False).start()
        fwd[kind, mine] = send[kind, owned]

    def add_column(kind):
        for step in range(1, 16):
            forward(kind, step, True).wait_recv()
        run = zeros
        for d in range(16) if kind == 0 else reversed(range(16)):
            ret[kind, d] = run
            run = run + fwd[kind, d]
        total[kind] = run
        for step in range(1, 16):
            pl.when(ahead(kind, step))(across(kind, step, False).start)

    def add_plane(kind):
        for step in range(1, 16):
            pl.when(ahead(1 - kind, step))(across(kind, step, True).wait_recv)
        entering = zeros
        for n in range(16):
            passed = n < chip if kind == 0 else n > chip
            entering = entering + jnp.where(passed, plane[kind, n], 0.0)
        for d in range(16):
            ret[kind, d] = ret[kind, d] + entering
        for step in range(1, 16):
            returned(kind, step, False).start()
        back[kind, owned] = ret[kind, mine]

    scale[...] = token_scale(group * 8 + z, (TOK, 128))
    loads[0].wait()
    loads[1].wait()

    def key_states(p, _):
        at = lanes_of(p)
        s = compact(dot(k[:, at], v[:, at], TN))
        send[0, 2 * p] = s[0:32]
        send[0, 2 * p + 1] = s[32:64]
        return 0

    lax.fori_loop(0, PAIRS, key_states, 0)
    pl.semaphore_wait(barrier, 30)
    send_slices(0)
    loads[2].wait()
    loads[3].wait()

    def query_states(p, _):
        at = lanes_of(p)
        c = scale[...]
        scaled = (q[:, at].astype(F32) * c).astype(BF16)
        qc[:, at] = scaled
        gc[:, at] = (g[:, at].astype(F32) * c).astype(BF16)
        r = compact(dot(scaled, g[:, at], TN))
        send[1, 2 * p] = r[0:32]
        send[1, 2 * p + 1] = r[32:64]
        return 0

    lax.fori_loop(0, PAIRS, query_states, 0)
    send_slices(1)

    def inside(p, _):
        at = lanes_of(p)
        causal = lax.broadcasted_iota(jnp.int32, (CHUNK, 2 * CHUNK), 0) >= (
            lax.broadcasted_iota(jnp.int32, (CHUNK, 2 * CHUNK), 1) % CHUNK
        )
        state = None
        later = [None] * CHUNKS
        running = None
        for n in reversed(range(1, CHUNKS)):
            rows = pl.ds(n * CHUNK, CHUNK)
            more = dot(qc[rows, at], g[rows, at], TN)
            running = more if running is None else running + more
            later[n - 1] = running
        for n in range(CHUNKS):
            rows = pl.ds(n * CHUNK, CHUNK)
            q_n, k_n, v_n, g_n = q[rows, at], k[rows, at], v[rows, at], g[rows, at]
            qc_n, gc_n = qc[rows, at], gc[rows, at]
            k_two, v_two = both_heads(k_n), both_heads(v_n)
            q_two, g_two = both_heads(q_n), both_heads(g_n)
            weights = jnp.where(causal, dot(qc_n, k_two, NT), 0.0).astype(BF16)
            backs = jnp.where(causal, dot(gc_n, v_two, NT), 0.0).astype(BF16)
            w_rows = jnp.concatenate([weights[:, :CHUNK], weights[:, CHUNK:]], axis=0)
            b_rows = jnp.concatenate([backs[:, :CHUNK], backs[:, CHUNK:]], axis=0)
            sums = [
                dot(weights, v_two, NN),
                dot(backs, k_two, NN),
                dot(b_rows, q_two, TN),
                dot(w_rows, g_two, TN),
            ]
            if n:
                s = diagonal(state).astype(BF16)
                sums[0] = sums[0] + dot(qc_n, s, NN)
                sums[1] = sums[1] + dot(gc_n, s, NT)
            if n < CHUNKS - 1:
                r = diagonal(later[n]).astype(BF16)
                sums[2] = sums[2] + dot(v_n, r, NT)
                sums[3] = sums[3] + dot(k_n, r, NN)
                more = dot(k_n, v_n, TN)
                state = more if state is None else state + more
            for i, x in enumerate(sums):
                part[p, i, rows] = x
        return 0

    def entered(kind, p):
        rows = [back[kind, 2 * p], back[kind, 2 * p + 1]]
        return diagonal(jnp.concatenate(rows * 2, axis=0)).astype(BF16)

    def finish_states(p, _):
        at = lanes_of(p)
        s = entered(0, p)
        c = scale[...]
        attended[:, at] = (part[p, 0] + c * dot(q[:, at], s, NN)).astype(BF16)
        grad_q[:, at] = (part[p, 1] + c * dot(g[:, at], s, NT)).astype(BF16)
        return 0

    def finish_adjoints(p, _):
        at = lanes_of(p)
        r = entered(1, p)
        grad_k[:, at] = (part[p, 2] + dot(v[:, at], r, NT)).astype(BF16)
        grad_v[:, at] = (part[p, 3] + dot(k[:, at], r, NN)).astype(BF16)
        return 0

    lax.fori_loop(0, 5, inside, 0)
    add_column(0)
    lax.fori_loop(5, 8, inside, 0)
    add_column(1)
    add_plane(0)
    add_plane(1)
    for step in range(1, 16):
        returned(0, step, True).wait_recv()
    lax.fori_loop(0, PAIRS, finish_states, 0)
    for kind in range(2):
        for step in range(1, 16):
            forward(kind, step, False).wait_send()
            pl.when(ahead(kind, step))(across(kind, step, False).wait_send)
            returned(kind, step, False).wait_send()
    for step in range(1, 16):
        returned(1, step, True).wait_recv()
    lax.fori_loop(0, PAIRS, finish_adjoints, 0)


def store_kernel(*refs):
    sources, targets, sem = refs[:4], refs[4:8], refs[8]
    half = TOK // 2
    copies = [
        pltpu.make_async_copy(src.at[pl.ds(h * half, half)], dst.at[pl.ds(h * half, half)], sem.at[2 * i + h])
        for i, (src, dst) in enumerate(zip(sources, targets))
        for h in range(2)
    ]
    for copy in copies:
        copy.start()
    for copy in copies:
        copy.wait()


def on_device(queries, keys, values, cotangent):
    hbm = pl.BlockSpec(memory_space=pltpu.HBM)
    vmem = pl.BlockSpec(memory_space=pltpu.VMEM)
    dma = pltpu.SemaphoreType.DMA
    tokens = pltpu.VMEM((TOK, COLS), BF16)
    slices = pltpu.VMEM((2, 16, 32, 128), F32)
    results = pl.pallas_call(
        attention_kernel,
        name="attention",
        out_shape=(jax.ShapeDtypeStruct((TOK, COLS), BF16),) * 4,
        in_specs=[hbm] * 4,
        out_specs=(vmem,) * 4,
        scratch_shapes=[tokens] * 6
        + [
            pltpu.VMEM((TOK, 128), F32),
            pltpu.VMEM((PAIRS, 4, TOK, 128), F32),
            slices,
            slices,
            pltpu.VMEM((2, 32, 128), F32),
            slices,
            slices,
            slices,
            dma((4,)),
        ]
        + [dma((2, 16))] * 6,
        compiler_params=pltpu.CompilerParams(
            collective_id=0, has_side_effects=True, vmem_limit_bytes=40 << 20
        ),
    )(*(pltpu.with_memory_space_constraint(x, pltpu.HBM) for x in (queries, keys, values, cotangent)))
    return pl.pallas_call(
        store_kernel,
        name="store",
        out_shape=(jax.ShapeDtypeStruct((TOK, COLS), BF16),) * 4,
        in_specs=[pl.BlockSpec(memory_space=pl.ANY)] * 4,
        out_specs=(pl.BlockSpec(memory_space=pl.ANY),) * 4,
        scratch_shapes=[dma((8,))],
        compiler_params=pltpu.CompilerParams(vmem_limit_bytes=8 << 20),
    )(*results)


def solution(mesh):
    placed = P(("major", "minor"), None)
    return jax.shard_map(
        on_device, mesh=mesh, in_specs=(placed,) * 4, out_specs=(placed,) * 4, check_vma=False
    )
```

```python
import jax
import jax.numpy as jnp
from jax import lax
from jax.experimental import pallas as pl
from jax.experimental.pallas import tpu as pltpu
from jax.sharding import PartitionSpec as P

TOK = 512
COLS = 1024
PAIRS = 8
CHUNK = 128
CHUNKS = TOK // CHUNK
F32 = jnp.float32
BF16 = jnp.bfloat16
MESH = pl.DeviceIdType.MESH

NT = (((1,), (1,)), ((), ()))
NN = (((1,), (0,)), ((), ()))
TN = (((0,), (0,)), ((), ()))


def dot(a, b, dims):
    return lax.dot_general(a, b, dims, preferred_element_type=F32)


def lanes_of(pair):
    return pl.ds(pl.multiple_of(pair * 128, 128), 128)


def token_scale(block, shape):
    pos = block * TOK + lax.broadcasted_iota(jnp.int32, shape, 0)
    return 1.0 / jnp.sqrt(pos.astype(F32) + 1.0)


def both_heads(x):
    low = lax.broadcasted_iota(jnp.int32, x.shape, 1) < 64
    zero = jnp.zeros_like(x)
    return jnp.concatenate([jnp.where(low, x, zero), jnp.where(low, zero, x)], axis=0)


def diagonal(x):
    row = lax.broadcasted_iota(jnp.int32, x.shape, 0) < 64
    col = lax.broadcasted_iota(jnp.int32, x.shape, 1) < 64
    return jnp.where(row == col, x, jnp.zeros_like(x))


def compact(x):
    low = lax.broadcasted_iota(jnp.int32, (64, 128), 1) < 64
    return jnp.where(low, x[0:64], x[64:128])


def attention_kernel(
    q_hbm, k_hbm, v_hbm, g_hbm, attended, grad_q, part_kv, k, v, adjoint,
    q, g, qc, scale, part, local, twin, low, both, f_low, f_both, total, plane, ret, back, other,
    in_sem, xs_sem, xr_sem, fs_sem, fr_sem, ps_sem, pr_sem, rs_sem, rr_sem, os_sem, or_sem,
):
    z = lax.axis_index("minor")
    group = lax.axis_index("major")
    core = lax.rem(group, 2)
    chip = group // 2
    zeros = jnp.zeros((32, 128), F32)
    sibling = {"minor": z, "major": chip * 2 + 1 - core}

    def up(step):
        return lax.rem(z + step, 8)

    def in_column(step):
        return {"minor": up(step), "major": group}

    def in_plane(step):
        return {"minor": z, "major": lax.rem(chip + step, 16) * 2 + core}

    loads = []
    for n, half in enumerate((1 - core, core)):
        cols = pl.ds(pl.multiple_of(half * 512, 512), 512)
        for m, (src, dst) in enumerate(((k_hbm, k), (v_hbm, v), (q_hbm, q), (g_hbm, g))):
            loads.append(pltpu.make_async_copy(src.at[:, cols], dst.at[:, cols], in_sem.at[n * 4 + m]))
    for n in (0, 1, 4, 5, 2, 3, 6, 7):
        loads[n].start()

    barrier = pltpu.get_barrier_semaphore()
    pl.semaphore_signal(barrier, inc=1, device_id=sibling, device_id_type=MESH)
    for step in range(1, 8):
        pl.semaphore_signal(barrier, inc=1, device_id=in_column(step), device_id_type=MESH)
    for step in range(1, 16):
        pl.semaphore_signal(barrier, inc=1, device_id=in_plane(step), device_id_type=MESH)

    def remote(src, dst, sent, landed, target):
        return pltpu.make_async_remote_copy(
            src_ref=src, dst_ref=dst, send_sem=sent, recv_sem=landed, device_id=target, device_id_type=MESH
        )

    def swap(kind):
        return remote(local.at[kind, 1 - core], twin.at[kind], xs_sem.at[kind], xr_sem.at[kind], sibling)

    def forward(kind, which, step, peer):
        src, dst = ((both, f_both), (low, f_low))[which]
        n = 2 * which + kind
        slot = up(step) if peer else z
        return remote(
            src.at[kind, up(step)], dst.at[kind, slot], fs_sem.at[n, step], fr_sem.at[n, slot], in_column(step)
        )

    def across(kind, step, peer):
        slot = lax.rem(chip + step, 16) if peer else chip
        return remote(
            total.at[kind], plane.at[kind, slot], ps_sem.at[kind, step], pr_sem.at[kind, slot], in_plane(step)
        )

    def returned(kind, step, peer):
        slot = up(step) if peer else z
        return remote(
            ret.at[kind, up(step)], back.at[kind, slot], rs_sem.at[kind, step], rr_sem.at[kind, slot], in_column(step)
        )

    def handed(kind, m):
        two = pl.ds(2 * m, 2)
        return remote(
            back.at[kind, two, 1 - core], other.at[kind, two], os_sem.at[kind, m], or_sem.at[kind, m], sibling
        )

    def ahead(kind, step):
        there = lax.rem(chip + step, 16)
        return there > chip if kind == 0 else there < chip

    def key_states(half):
        def body(m, _):
            at = lanes_of(half * 4 + m)
            s = compact(dot(k[:, at], v[:, at], TN))
            local[0, half, 2 * m] = s[0:32]
            local[0, half, 2 * m + 1] = s[32:64]
            return 0

        lax.fori_loop(0, 4, body, 0, unroll=True)

    def query_states(half):
        def body(m, _):
            at = lanes_of(half * 4 + m)
            scaled = (q[:, at].astype(F32) * scale[...]).astype(BF16)
            qc[:, at] = scaled
            r = compact(dot(scaled, g[:, at], TN))
            local[1, half, 2 * m] = r[0:32]
            local[1, half, 2 * m + 1] = r[32:64]
            return 0

        lax.fori_loop(0, 4, body, 0, unroll=True)

    def send_slices(kind):
        swap(kind).wait_recv()
        for j in range(8):
            own, theirs = local[kind, core, j], twin[kind, j]
            both[kind, j] = own + theirs
            low[kind, j] = jnp.where(core == 0, own, theirs)
        for step in range(1, 8):
            forward(kind, 0, step, False).start()
        f_both[kind, z] = both[kind, z]
        f_low[kind, z] = low[kind, z]

    def add_column(kind):
        for step in range(1, 8):
            forward(kind, 0, step, True).wait_recv()
        run = zeros
        for j in range(8):
            run = run + f_both[kind, j]
        total[kind] = run
        for step in range(1, 16):
            pl.when(ahead(kind, step))(across(kind, step, False).start)

    def add_blocks(kind):
        for step in range(1, 8):
            forward(kind, 1, step, True).wait_recv()
        order = list(range(8)) if kind == 0 else list(reversed(range(8)))
        run = zeros
        for part_of in (0, 1) if kind == 0 else (1, 0):
            for j in order:
                ret[kind, j, part_of] = run
                piece = f_low[kind, j]
                run = run + (piece if part_of == 0 else f_both[kind, j] - piece)

    def add_plane(kind):
        for step in range(1, 16):
            pl.when(ahead(1 - kind, step))(across(kind, step, True).wait_recv)
        entering = zeros
        for n in range(16):
            passed = n < chip if kind == 0 else n > chip
            entering = entering + jnp.where(passed, plane[kind, n], 0.0)
        for step in range(8):
            j = up(step)
            for part_of in range(2):
                ret[kind, j, part_of] = ret[kind, j, part_of] + entering
            if step:
                returned(kind, step, False).start()
        back[kind, z] = ret[kind, z]

    scale[...] = token_scale(group * 8 + z, (TOK, 128))
    for n in (0, 1, 4, 5):
        loads[n].wait()
    key_states(1 - core)
    key_states(core)
    for n in (2, 3, 6, 7):
        loads[n].wait()
    query_states(1 - core)
    query_states(core)
    pl.semaphore_wait(barrier, 23)
    swap(0).start()
    swap(1).start()
    send_slices(0)
    send_slices(1)
    for kind in range(2):
        for step in range(1, 8):
            forward(kind, 1, step, False).start()

    def inside(p, _):
        at = lanes_of(p)
        causal = lax.broadcasted_iota(jnp.int32, (CHUNK, 2 * CHUNK), 0) >= (
            lax.broadcasted_iota(jnp.int32, (CHUNK, 2 * CHUNK), 1) % CHUNK
        )
        state = None
        later = [None] * CHUNKS
        running = None
        for n in reversed(range(1, CHUNKS)):
            rows = pl.ds(n * CHUNK, CHUNK)
            more = dot(qc[rows, at], g[rows, at], TN)
            running = more if running is None else running + more
            later[n - 1] = running
        for n in range(CHUNKS):
            rows = pl.ds(n * CHUNK, CHUNK)
            q_n, k_n, v_n, g_n = q[rows, at], k[rows, at], v[rows, at], g[rows, at]
            qc_n = qc[rows, at]
            gc_n = (g_n.astype(F32) * scale[rows]).astype(BF16)
            k_two, v_two = both_heads(k_n), both_heads(v_n)
            q_two, g_two = both_heads(q_n), both_heads(g_n)
            weights = jnp.where(causal, dot(qc_n, k_two, NT), 0.0).astype(BF16)
            backs = jnp.where(causal, dot(gc_n, v_two, NT), 0.0).astype(BF16)
            w_rows = jnp.concatenate([weights[:, :CHUNK], weights[:, CHUNK:]], axis=0)
            b_rows = jnp.concatenate([backs[:, :CHUNK], backs[:, CHUNK:]], axis=0)
            sums = [
                dot(weights, v_two, NN),
                dot(backs, k_two, NN),
                dot(b_rows, q_two, TN),
                dot(w_rows, g_two, TN),
            ]
            if n:
                s = diagonal(state).astype(BF16)
                sums[0] = sums[0] + dot(qc_n, s, NN)
                sums[1] = sums[1] + dot(gc_n, s, NT)
            if n < CHUNKS - 1:
                r = diagonal(later[n]).astype(BF16)
                sums[2] = sums[2] + dot(v_n, r, NT)
                sums[3] = sums[3] + dot(k_n, r, NN)
                more = dot(k_n, v_n, TN)
                state = more if state is None else state + more
            for i, x in enumerate(sums):
                if i < 2:
                    part[p, i, rows] = x
                else:
                    part_kv[p, i - 2, rows] = x
        return 0


    def finish(kind, p, rows):
        if kind == 0:
            at = lanes_of(p)
            x = diagonal(jnp.concatenate(rows * 2, axis=0)).astype(BF16)
            c = scale[...]
            attended[:, at] = (part[p, 0] + c * dot(q[:, at], x, NN)).astype(BF16)
            grad_q[:, at] = (part[p, 1] + c * dot(g[:, at], x, NT)).astype(BF16)
        else:
            adjoint[p, 0:32] = rows[0]
            adjoint[p, 32:64] = rows[1]

    def turn(i):
        return lax.rem(z // 2 + i + i // 2 - 2 * (i // 3), 4)

    def arrived(kind, j):
        step = lax.rem(j - z + 8, 8)
        pl.when(j != z)(returned(kind, step, True).wait_recv)

    def finish_own(kind):
        def body(i, _):
            m = turn(i)
            arrived(kind, 2 * m)
            arrived(kind, 2 * m + 1)
            handed(kind, m).start()
            finish(kind, core * 4 + m, [back[kind, 2 * m, core], back[kind, 2 * m + 1, core]])
            return 0

        lax.fori_loop(0, 4, body, 0)

    def finish_other(kind):
        def body(i, _):
            m = turn(i)
            handed(kind, m).wait_recv()
            finish(kind, (1 - core) * 4 + m, [other[kind, 2 * m], other[kind, 2 * m + 1]])
            return 0

        lax.fori_loop(0, 4, body, 0)

    lax.fori_loop(0, 3, inside, 0)
    add_column(0)
    add_column(1)
    lax.fori_loop(3, 5, inside, 0)
    add_blocks(0)
    add_blocks(1)
    add_plane(0)
    add_plane(1)
    lax.fori_loop(5, 8, inside, 0)
    finish_own(0)
    finish_other(0)
    for kind in range(2):
        swap(kind).wait_send()
        for step in range(1, 8):
            forward(kind, 0, step, False).wait_send()
            forward(kind, 1, step, False).wait_send()
            returned(kind, step, False).wait_send()
        for step in range(1, 16):
            pl.when(ahead(kind, step))(across(kind, step, False).wait_send)
    finish_own(1)
    finish_other(1)
    for kind in range(2):
        for m in range(4):
            handed(kind, m).wait_send()


def store_kernel(attended, grad_q, part_kv, k, v, adjoint, a_hbm, q_hbm, k_hbm, v_hbm, k_out, v_out, sem, kv_sem):
    half = TOK // 2
    copies = [
        pltpu.make_async_copy(src.at[pl.ds(h * half, half)], dst.at[pl.ds(h * half, half)], sem.at[2 * i + h])
        for i, (src, dst) in enumerate(((attended, a_hbm), (grad_q, q_hbm)))
        for h in range(2)
    ]
    for copy in copies:
        copy.start()
    for p in range(PAIRS):
        at = pl.ds(p * 128, 128)
        x = diagonal(jnp.concatenate([adjoint[p]] * 2, axis=0)).astype(BF16)
        k_out[:, at] = (part_kv[p, 0] + dot(v[:, at], x, NT)).astype(BF16)
        v_out[:, at] = (part_kv[p, 1] + dot(k[:, at], x, NN)).astype(BF16)
        if p % 2:
            cols = pl.ds(p * 128 - 128, 256)
            for i, (src, dst) in enumerate(((k_out, k_hbm), (v_out, v_hbm))):
                copies.append(pltpu.make_async_copy(src.at[:, cols], dst.at[:, cols], kv_sem.at[i, p // 2]))
                copies[-1].start()
    for copy in copies:
        copy.wait()


def on_device(queries, keys, values, cotangent):
    hbm = pl.BlockSpec(memory_space=pltpu.HBM)
    vmem = pl.BlockSpec(memory_space=pltpu.VMEM)
    anywhere = pl.BlockSpec(memory_space=pl.ANY)
    dma = pltpu.SemaphoreType.DMA
    tokens = pltpu.VMEM((TOK, COLS), BF16)
    out = jax.ShapeDtypeStruct((TOK, COLS), BF16)

    def slices(*lead):
        return pltpu.VMEM((*lead, 32, 128), F32)

    results = pl.pallas_call(
        attention_kernel,
        name="attention",
        out_shape=(
            out,
            out,
            jax.ShapeDtypeStruct((PAIRS, 2, TOK, 128), F32),
            out,
            out,
            jax.ShapeDtypeStruct((PAIRS, 64, 128), F32),
        ),
        in_specs=[hbm] * 4,
        out_specs=(vmem,) * 6,
        scratch_shapes=[tokens] * 3
        + [
            pltpu.VMEM((TOK, 128), F32),
            pltpu.VMEM((PAIRS, 2, TOK, 128), F32),
            slices(2, 2, 8),
            slices(2, 8),
            slices(2, 8),
            slices(2, 8),
            slices(2, 8),
            slices(2, 8),
            slices(2),
            slices(2, 16),
            slices(2, 8, 2),
            slices(2, 8, 2),
            slices(2, 8),
            dma((8,)),
            dma((2,)),
            dma((2,)),
            dma((4, 8)),
            dma((4, 8)),
            dma((2, 16)),
            dma((2, 16)),
            dma((2, 8)),
            dma((2, 8)),
            dma((2, 4)),
            dma((2, 4)),
        ],
        compiler_params=pltpu.CompilerParams(
            collective_id=0, has_side_effects=True, vmem_limit_bytes=32 << 20
        ),
    )(*(pltpu.with_memory_space_constraint(x, pltpu.HBM) for x in (queries, keys, values, cotangent)))
    return pl.pallas_call(
        store_kernel,
        name="store",
        out_shape=(out,) * 4,
        in_specs=[anywhere] * 2 + [vmem] * 4,
        out_specs=(anywhere,) * 4,
        scratch_shapes=[tokens, tokens, dma((4,)), dma((2, 4))],
        compiler_params=pltpu.CompilerParams(vmem_limit_bytes=16 << 20),
    )(*results)


def solution(mesh):
    placed = P(("major", "minor"), None)
    return jax.shard_map(
        on_device, mesh=mesh, in_specs=(placed,) * 4, out_specs=(placed,) * 4, check_vma=False
    )
```
